128 devices in a mesh: depth: 4 (over y), row: 8 (over x_lo, z), col: 4 (over x_hi, core).
Axes of the slice: x: 4 (x_hi: 2, x_lo: 2; x = x_hi * 2 + x_lo), y: 4, z: 4, core: 2. Of those that a mesh axis runs over, the one named last changes fastest.
Arguments:
- tokens: bfloat16 [768, 8192], P(('row', 'col'), 'depth'), may hold values from -6 to 6
- cotangent: bfloat16 [768, 8192], P(('row', 'col'), 'depth'), may hold values from -6 to 6
- gate_weight: bfloat16 [8192, 28672], P('depth', ('row', 'col')), may hold values from -0.0625 to 0.0625
- up_weight: bfloat16 [8192, 28672], P('depth', ('row', 'col')), may hold values from -0.0625 to 0.0625
- down_weight: bfloat16 [28672, 8192], P(('row', 'col'), 'depth'), may hold values from -0.03125 to 0.03125
Outputs:
- tokens_grad: bfloat16 [768, 8192], P(('row', 'col'), 'depth')
- gate_grad: bfloat16 [8192, 28672], P('depth', ('row', 'col'))
- up_grad: bfloat16 [8192, 28672], P('depth', ('row', 'col'))
- down_grad: bfloat16 [28672, 8192], P(('row', 'col'), 'depth')
The draws below stay inside these ranges and needn't reach their ends.
All inputs are finite; a program needn't handle non-finite values.
Results may differ from the reference program's by a relative error of at most 0.005.
Values may be sent and summed in bfloat16 or wider, within the bound.
No kernel may reach another device: no remote copies, remote signals or barrier semaphores. Data moves between devices by JAX's collectives and lax.ppermute only.
A program may use at most 128 MiB of HBM per device.

```python
import jax
import jax.numpy as jnp
from jax import lax

D = 8192
FF = 28672
TOKENS = 768


def steps_of(rng, shape, cuts, low, largest):
    loudness, own = 1.0, jax.random.fold_in(rng, 6)
    for dim, shards_of in cuts:
        draws = jnp.exp(jax.random.uniform(jax.random.fold_in(own, dim), (shards_of,), jnp.float32, low / len(cuts), largest / len(cuts)))
        loudness = loudness * jnp.repeat(draws, shape[dim] // shards_of).reshape([-1 if axis == dim else 1 for axis in range(len(shape))])
    return loudness


def normal_values(own_key, extent, width, bound, shards=(), dtype=jnp.bfloat16):
    factor_of = steps_of(own_key, extent, shards, -0.22, 0.18) if shards else 1.0
    array = jax.random.normal(own_key, extent, jnp.float32) * width * factor_of
    return jnp.minimum(jnp.maximum(array, -bound), bound).astype(dtype)


def setup_inputs(seed: int = 0) -> dict:
    keys = jax.random.split(jax.random.key(seed), 6)
    tokens = normal_values(keys[0], (TOKENS, D), 1.0, 6.0, ((0, 32), (1, 4)))
    cotangent = normal_values(keys[1], (TOKENS, D), 1.0, 6.0, ((0, 32), (1, 4)))
    gate_weight = normal_values(keys[2], (D, FF), D ** -0.5, 0.0625, ((0, 4), (1, 32)))
    up_weight = normal_values(keys[3], (D, FF), D ** -0.5, 0.0625, ((0, 4), (1, 32)))
    down_weight = normal_values(keys[4], (FF, D), FF ** -0.5, 0.03125, ((0, 32), (1, 4)))
    return dict(tokens=tokens, cotangent=cotangent, gate_weight=gate_weight, up_weight=up_weight, down_weight=down_weight)


def inner(left, right):
    return lax.dot_general(left, right, (((0,), (0,)), ((), ())), preferred_element_type=jnp.float32)


def outer(left, right):
    return lax.dot_general(left, right, (((1,), (1,)), ((), ())), preferred_element_type=jnp.float32)


def reference(tokens, cotangent, gate_weight, up_weight, down_weight):
    gate = jnp.dot(tokens, gate_weight, preferred_element_type=jnp.float32)
    up = jnp.dot(tokens, up_weight, preferred_element_type=jnp.float32)
    hidden_grad = outer(cotangent, down_weight)
    sigma = jax.nn.sigmoid(gate)
    active = gate * sigma
    hidden = (active * up).astype(jnp.bfloat16)
    gate_delta = (hidden_grad * up * sigma * (1.0 + gate * (1.0 - sigma))).astype(jnp.bfloat16)
    up_delta = (hidden_grad * active).astype(jnp.bfloat16)
    down_grad = inner(hidden, cotangent).astype(jnp.bfloat16)
    gate_grad = inner(tokens, gate_delta).astype(jnp.bfloat16)
    up_grad = inner(tokens, up_delta).astype(jnp.bfloat16)
    tokens_grad = (outer(gate_delta, gate_weight) + outer(up_delta, up_weight)).astype(jnp.bfloat16)
    return tokens_grad, gate_grad, up_grad, down_grad
```

```python
import jax
import jax.numpy as jnp
from jax import lax
from jax.sharding import PartitionSpec as P

ALL = ("depth", "row", "col")
BF = jnp.bfloat16
F32 = jnp.float32


def place(y, x, z, core):
    x, y, z = x % 4, y % 4, z % 4
    return (y * 8 + (x % 2) * 4 + z) * 4 + (x // 2) * 2 + core


def links(source):
    pairs = []
    for y in range(4):
        for x in range(4):
            for z in range(4):
                for core in range(2):
                    pairs.append((place(*source(y, x, z, core)), place(y, x, z, core)))
    return pairs


def from_z(a, k):
    return lax.ppermute(a, ALL, links(lambda y, x, z, c: (y, x, z + k, c)))


def from_x(a, k):
    return lax.ppermute(a, ALL, links(lambda y, x, z, c: (y, x + k, z, c)))


def from_x_turned(a, k):
    return lax.ppermute(a, ALL, links(lambda y, x, z, c: (y, x + y + k, z, c)))


def to_x_turned(a, k):
    return lax.ppermute(a, ALL, links(lambda y, x, z, c: (y, x - y - k, z, c)))


def from_y(a, k):
    return lax.ppermute(a, ALL, links(lambda y, x, z, c: (y + k, x, z, c)))


def other_core(a):
    return lax.ppermute(a, ALL, links(lambda y, x, z, c: (y, x, z, 1 - c)))


def outer(left, right):
    return lax.dot_general(left, right, (((1,), (1,)), ((), ())), preferred_element_type=F32)


def inner(left, right):
    return lax.dot_general(left, right, (((0,), (0,)), ((), ())), preferred_element_type=F32)


def dot(left, right):
    return jnp.dot(left, right, preferred_element_type=F32)


def cat(*parts, axis=0):
    return jnp.concatenate(parts, axis=axis)


def sum_depth(blocks, own):
    half = blocks[2].shape[0] // 2
    via_up = from_y(blocks[2][:half], -1)
    via_down = from_y(blocks[2][half:], 1)
    up = cat((blocks[1][:half].astype(F32) + via_up.astype(F32)).astype(BF), blocks[1][half:])
    down = cat(blocks[3][:half], (blocks[3][half:].astype(F32) + via_down.astype(F32)).astype(BF))
    return own + from_y(up, -1).astype(F32) + from_y(down, 1).astype(F32)


def spread_depth(a):
    half = a.shape[0] // 2
    before, after = from_y(a, -1), from_y(a, 1)
    across = cat(from_y(before[:half], -1), from_y(after[half:], 1))
    return [a, after, across, before]


def pointwise(gate, up, hidden_grad):
    sigma = jax.nn.sigmoid(gate)
    active = gate * sigma
    hidden = (active * up).astype(BF)
    gate_delta = (hidden_grad * up * sigma * (1.0 + gate * (1.0 - sigma))).astype(BF)
    up_delta = (hidden_grad * active).astype(BF)
    return hidden, gate_delta, up_delta


def body(tokens, cotangent, gate_weight, up_weight, down_weight):
    tz = [tokens] + [from_z(tokens, k) for k in (1, 2, 3)]
    cx = [from_x_turned(cotangent, k) for k in range(4)]
    tz = cat(*tz)
    tok_own = cat(*[from_x_turned(tz, k) for k in range(4)])
    cx = cat(*cx)
    cz = jnp.stack([cx] + [from_z(cx, k) for k in (1, 2, 3)])
    cot_own = cz.reshape(4, 4, 24, 2048).transpose(1, 0, 2, 3).reshape(384, 2048)
    tok = [tok_own, other_core(tok_own)]
    cot = [cot_own, other_core(cot_own)]

    gate, up, back = [], [], []
    for half in range(2):
        g, u = dot(tok[half], gate_weight), dot(tok[half], up_weight)
        parts = [cat(g[96 * k : 96 * k + 96], u[96 * k : 96 * k + 96], axis=1) for k in range(4)]
        both = sum_depth([p.astype(BF) for p in parts], parts[0])
        gate.append(both[:, :896])
        up.append(both[:, 896:])
    h = [outer(cot[half], down_weight) for half in range(2)]
    parts = [cat(h[0][96 * k : 96 * k + 96], h[1][96 * k : 96 * k + 96]) for k in range(4)]
    back = sum_depth([p.astype(BF) for p in parts], parts[0])

    hidden, delta, partial = [None, None], [None, None], [None, None]
    for half in (1, 0):
        hidden[half], gate_delta, up_delta = pointwise(gate[half], up[half], back[96 * half : 96 * half + 96])
        delta[half] = cat(*spread_depth(cat(gate_delta, up_delta, axis=1)))
    hidden = spread_depth(cat(*hidden))

    for half in (1, 0):
        partial[half] = outer(delta[half][:, :896], gate_weight) + outer(delta[half][:, 896:], up_weight)
    own = partial[0] + other_core(partial[1])
    own_bf = own.astype(BF)
    total = sum(to_x_turned(own_bf[96 * k : 96 * k + 96], k).astype(F32) for k in range(4))
    tokens_grad = total[:24] + sum(from_z(total[24 * k : 24 * k + 24], -k) for k in (1, 2, 3))

    tok, cot = cat(*tok), cat(*cot)
    hidden = cat(*[b[:96] for b in hidden], *[b[96:] for b in hidden])
    delta = cat(*delta)
    gate_grad = inner(tok, delta[:, :896]).astype(BF)
    up_grad = inner(tok, delta[:, 896:]).astype(BF)
    down_grad = inner(hidden, cot).astype(BF)
    return tokens_grad.astype(BF), gate_grad, up_grad, down_grad


def solution(mesh):
    act, weight, turned = P(("row", "col"), "depth"), P("depth", ("row", "col")), P(("row", "col"), "depth")
    return jax.shard_map(
        body, mesh=mesh, in_specs=(act, act, weight, weight, turned), out_specs=(act, weight, weight, turned), check_vma=False
    )
```

```python
import jax
import jax.numpy as jnp
from jax import lax
from jax.sharding import PartitionSpec as P

ALL = ("depth", "row", "col")
BF = jnp.bfloat16
F32 = jnp.float32


def place(y, x, z, core):
    x, y, z = x % 4, y % 4, z % 4
    return (y * 8 + (x % 2) * 4 + z) * 4 + (x // 2) * 2 + core


def pull(a, source):
    pairs = []
    for y in range(4):
        for x in range(4):
            for z in range(4):
                for core in range(2):
                    pairs.append((place(*source(y, x, z, core)), place(y, x, z, core)))
    return lax.ppermute(a, ALL, pairs)


def near(a, k):
    return pull(a, lambda y, x, z, c: (y, x + k * c, z + k * (1 - c), c))


def far(a, k):
    return pull(a, lambda y, x, z, c: (y, x + k * (1 - c), z + k * c, c))


def from_y(a, k):
    return pull(a, lambda y, x, z, c: (y + k, x, z, c))


def other_core(a):
    return pull(a, lambda y, x, z, c: (y, x, z, 1 - c))


def outer(left, right):
    return lax.dot_general(left, right, (((1,), (1,)), ((), ())), preferred_element_type=F32)


def inner(left, right):
    return lax.dot_general(left, right, (((0,), (0,)), ((), ())), preferred_element_type=F32)


def dot(left, right):
    return jnp.dot(left, right, preferred_element_type=F32)


def cat(*parts, axis=0):
    return jnp.concatenate(parts, axis=axis)


def together(*arrays):
    return lax.optimization_barrier(arrays)


def blocks_of(parts):
    n = parts[0].shape[0] // 96
    return lambda k: cat(*[p.reshape(n, 4, 24, 896)[:, k] for p in parts], axis=2).reshape(n * 24, 2688)


def first_step(block):
    across = block(2).astype(BF)
    half = across.shape[0] // 2
    return from_y(across[:half], -1), from_y(across[half:], 1)


def second_step(block, via_up, via_down):
    half = via_up.shape[0]
    up, down = block(1), block(3)
    up = cat((up[:half] + via_up.astype(F32)).astype(BF), up[half:].astype(BF))
    down = cat(down[:half].astype(BF), (down[half:] + via_down.astype(F32)).astype(BF))
    return up, down


def last_step(block, up, down):
    return block(0) + from_y(up, -1).astype(F32) + from_y(down, 1).astype(F32)


def by_row(*blocks):
    rows, width = blocks[0].shape
    return cat(*[b.reshape(rows // 24, 1, 24, width) for b in blocks], axis=1).reshape(rows * 4, width)


def pointwise(total):
    gate, up, hidden_grad = total[:, :896], total[:, 896:1792], total[:, 1792:]
    sigma = jax.nn.sigmoid(gate)
    active = gate * sigma
    hidden = (active * up).astype(BF)
    gate_delta = (hidden_grad * up * sigma * (1.0 + gate * (1.0 - sigma))).astype(BF)
    up_delta = (hidden_grad * active).astype(BF)
    return cat(hidden, gate_delta, up_delta, axis=1)


def spread(a):
    return from_y(a, -1), from_y(a, 1)


def spread_across(before, after):
    half = before.shape[0] // 2
    return cat(from_y(before[:half], -1), from_y(after[half:], 1))


def body(tokens, cotangent, gate_weight, up_weight, down_weight):
    y = lax.axis_index("depth")
    width = tokens.shape[1]

    def products(tok, cot):
        return [dot(tok, gate_weight), dot(tok, up_weight), outer(cot, down_weight)]

    def back_products(delta):
        return outer(delta[:, :896], gate_weight) + outer(delta[:, 896:], up_weight)

    tc = cat(tokens, cotangent)
    first = jnp.zeros((2, 4, 24, width), BF)
    for k, b in ((0, tc), (1, near(tc, 1)), (3, near(tc, 3)), (2, near(tc, 2))):
        first = lax.dynamic_update_slice_in_dim(first, b.reshape(2, 1, 24, width), lax.rem(k - y + 4, 4), 1)
    q0 = first.reshape(2, 96, width)
    q1, q3, q2 = far(q0, 1), far(q0, 3), far(q0, 2)
    qa = cat(q0, q1, q3, q2, axis=1)
    qb = other_core(qa)

    block_a = blocks_of(products(*qa))
    via_a = first_step(block_a)
    *part_b, via_up, via_down = together(*products(*qb), *via_a)
    block_b = blocks_of(part_b)
    via_b = first_step(block_b)
    up_a, down_a = second_step(block_a, via_up, via_down)
    up_b, down_b = second_step(block_b, *via_b)
    own = pointwise(last_step(block_a, up_a, down_a))
    other = pointwise(last_step(block_b, up_b, down_b))

    delta, hidden = cat(own[:, 896:], other[:, 896:]), cat(own[:, :896], other[:, :896])
    before_d, after_d, before_h, after_h = together(*spread(delta), *spread(hidden))
    across_d = spread_across(before_d, after_d)
    across_h = spread_across(before_h, after_h)
    delta = by_row(delta, after_d, across_d, before_d)
    hidden = by_row(hidden, after_h, across_h, before_h)

    part_other = other_core(back_products(delta[384:]))
    part = back_products(delta[:384]) + part_other
    part_bf, delta = together(part.astype(BF), delta)
    tok, cot = cat(qa[0], qb[0]), cat(qa[1], qb[1])
    gate_grad = inner(tok, delta[:, :896]).astype(BF)
    up_grad = inner(tok, delta[:, 896:]).astype(BF)
    gate_grad, up_grad, *parts = together(
        gate_grad, up_grad, *[far(part_bf[96 * n : 96 * n + 96], -k) for n, k in ((1, 1), (2, 3), (3, 2))]
    )
    total = part[:96] + sum(p.astype(F32) for p in parts)
    total, hidden = together(total, hidden)
    down_grad = inner(hidden, cot).astype(BF)

    def block(k):
        return lax.dynamic_slice_in_dim(total, lax.rem(k - y + 4, 4) * 24, 24, 0)

    tokens_grad = block(0) + sum(near(block(k), -k) for k in (1, 3, 2))
    return tokens_grad.astype(BF), gate_grad, up_grad, down_grad


def solution(mesh):
    act, weight, turned = P(("row", "col"), "depth"), P("depth", ("row", "col")), P(("row", "col"), "depth")
    return jax.shard_map(
        body, mesh=mesh, in_specs=(act, act, weight, weight, turned), out_specs=(act, weight, weight, turned), check_vma=False
    )
```

```python
import jax
import jax.numpy as jnp
from jax import lax
from jax.sharding import PartitionSpec as P

ALL = ("depth", "row", "col")
BF = jnp.bfloat16
F32 = jnp.float32


def place(y, x, z, core):
    x, y, z = x % 4, y % 4, z % 4
    return (y * 8 + (x % 2) * 4 + z) * 4 + (x // 2) * 2 + core


def pull(a, source):
    pairs = []
    for y in range(4):
        for x in range(4):
            for z in range(4):
                for core in range(2):
                    pairs.append((place(*source(y, x, z, core)), place(y, x, z, core)))
    return lax.ppermute(a, ALL, pairs)


def near(a, k):
    return pull(a, lambda y, x, z, c: (y, x + k * c, z + k * (1 - c), c))


def far(a, k):
    return pull(a, lambda y, x, z, c: (y, x + k * (1 - c), z + k * c, c))


def from_y(a, k):
    return pull(a, lambda y, x, z, c: (y + k, x, z, c))


def other_core(a):
    return pull(a, lambda y, x, z, c: (y, x, z, 1 - c))


def outer(left, right):
    return lax.dot_general(left, right, (((1,), (1,)), ((), ())), preferred_element_type=F32)


def inner(left, right):
    return lax.dot_general(left, right, (((0,), (0,)), ((), ())), preferred_element_type=F32)


def dot(left, right):
    return jnp.dot(left, right, preferred_element_type=F32)


def cat(*parts, axis=0):
    return jnp.concatenate(parts, axis=axis)


def together(*arrays):
    return lax.optimization_barrier(arrays)


def blocks_of(parts):
    n = parts[0].shape[0] // 96
    return lambda k: cat(*[p.reshape(n, 4, 24, -1)[:, k] for p in parts], axis=2).reshape(n * 24, 2688)


def first_step(block):
    across = block(2).astype(BF)
    half = (across.shape[0] // 2 + 7) // 8 * 8
    return from_y(across[:half], -1), from_y(across[half:], 1)


def second_step(block, via_up, via_down):
    half = via_up.shape[0]
    up, down = block(1), block(3)
    up = cat((up[:half] + via_up.astype(F32)).astype(BF), up[half:].astype(BF))
    down = cat(down[:half].astype(BF), (down[half:] + via_down.astype(F32)).astype(BF))
    return up, down


def last_step(block, up, down):
    return block(0) + from_y(up, -1).astype(F32) + from_y(down, 1).astype(F32)


def by_row(*blocks):
    rows, width = blocks[0].shape
    return cat(*[b.reshape(rows // 24, 1, 24, width) for b in blocks], axis=1).reshape(rows * 4, width)


def pointwise(total):
    gate, up, hidden_grad = total[:, :896], total[:, 896:1792], total[:, 1792:]
    sigma = jax.nn.sigmoid(gate)
    active = gate * sigma
    hidden = (active * up).astype(BF)
    gate_delta = (hidden_grad * up * sigma * (1.0 + gate * (1.0 - sigma))).astype(BF)
    up_delta = (hidden_grad * active).astype(BF)
    return cat(hidden, gate_delta, up_delta, axis=1)


def spread(a):
    return from_y(a, -1), from_y(a, 1)


def spread_across(before, after):
    half = before.shape[0] // 2
    return cat(from_y(before[:half], -1), from_y(after[half:], 1))


def body(tokens, cotangent, gate_weight, up_weight, down_weight):
    y = lax.axis_index("depth")
    width = tokens.shape[1]

    def products(tok, cot):
        return [dot(tok, weights), outer(cot, down_weight)]

    tc = cat(tokens, cotangent)
    weights = cat(gate_weight, up_weight, axis=1)
    near_2, near_1, near_3, weights = together(near(tc, 2), near(tc, 1), near(tc, 3), weights)
    first = jnp.zeros((2, 4, 24, width), BF)
    for k, b in ((2, near_2), (1, near_1), (3, near_3), (0, tc)):
        first = lax.dynamic_update_slice_in_dim(first, b.reshape(2, 1, 24, width), lax.rem(k - y + 4, 4), 1)
    q0 = first.reshape(2, 96, width)
    o0 = other_core(q0)
    q2, q1, q3 = far(q0, 2), far(q0, 1), far(q0, 3)
    tok_0, cot_0 = cat(q0[0], o0[0]), cat(q0[1], o0[1])
    block_0 = blocks_of(products(tok_0, cot_0))
    up_0, down_0 = second_step(block_0, *first_step(block_0))
    q2, q1, q3, up_0, down_0 = together(q2, q1, q3, up_0, down_0)

    tok_a, cot_a = [cat(*[q[n] for q in (q1, q3, q2)]) for n in range(2)]
    tok_b, cot_b = together(other_core(tok_a), other_core(cot_a))
    *part_a, up_0, down_0 = together(*products(tok_a, cot_a), from_y(up_0, -1), from_y(down_0, 1))
    block_a = blocks_of(part_a)
    via_a = first_step(block_a)
    part_b = products(tok_b, cot_b)
    block_b = blocks_of(part_b)
    via_b = first_step(block_b)
    *part_b, via_up, via_down = together(*part_b, *via_a)
    total_0 = block_0(0) + up_0.astype(F32) + down_0.astype(F32)
    up_a, down_a = second_step(block_a, via_up, via_down)
    up_b, down_b = second_step(block_b, *via_b)
    result_0 = pointwise(total_0)
    own = cat(result_0[:24], pointwise(last_step(block_a, up_a, down_a)))
    other = cat(result_0[24:], pointwise(last_step(blocks_of(part_b), up_b, down_b)))

    delta, hidden = cat(own[:, 896:], other[:, 896:]), cat(own[:, :896], other[:, :896])
    before_d, after_d = spread(delta)
    before_d, after_d, hidden = together(before_d, after_d, hidden)
    across_d = spread_across(before_d, after_d)
    delta = by_row(delta, after_d, across_d, before_d)
    before_h, after_h = spread(hidden)
    delta_own, before_h, after_h = together(delta[:384], before_h, after_h)
    hidden = by_row(hidden, after_h, spread_across(before_h, after_h), before_h)

    part_other = other_core(outer(delta[384:], weights).astype(BF))
    part_own, part_other = together(outer(delta_own, weights), part_other)
    part = part_own + part_other.astype(F32)
    part_bf, gate_delta, up_delta = together(part.astype(BF), delta[:, :896], delta[:, 896:])
    tok, cot = cat(tok_0[:96], tok_a, tok_0[96:], tok_b), cat(cot_0[:96], cot_a, cot_0[96:], cot_b)
    gate_grad = inner(tok, gate_delta).astype(BF)
    up_grad = inner(tok, up_delta).astype(BF)
    gate_grad, up_grad, *parts = together(
        gate_grad, up_grad, *[far(part_bf[96 * n : 96 * n + 96], -k) for n, k in ((3, 2), (1, 1), (2, 3))]
    )
    total = part[:96] + sum(p.astype(F32) for p in parts)
    total, hidden = together(total, hidden)
    down_grad = inner(hidden, cot).astype(BF)

    def block(k):
        return lax.dynamic_slice_in_dim(total, lax.rem(k - y + 4, 4) * 24, 24, 0)

    tokens_grad = block(0) + sum(near(block(k), -k) for k in (2, 1, 3))
    return tokens_grad.astype(BF), gate_grad, up_grad, down_grad


def solution(mesh):
    act, weight, turned = P(("row", "col"), "depth"), P("depth", ("row", "col")), P(("row", "col"), "depth")
    return jax.shard_map(
        body, mesh=mesh, in_specs=(act, act, weight, weight, turned), out_specs=(act, weight, weight, turned), check_vma=False
    )
```

```python
import jax
import jax.numpy as jnp
from jax import lax
from jax.experimental import pallas as pl
from jax.experimental.pallas import tpu as pltpu
from jax.sharding import PartitionSpec as P

ALL = ("depth", "row", "col")
BF = jnp.bfloat16
F32 = jnp.float32


def place(y, x, z, core):
    x, y, z = x % 4, y % 4, z % 4
    return (y * 8 + (x % 2) * 4 + z) * 4 + (x // 2) * 2 + core


def pull(a, source):
    pairs = []
    for y in range(4):
        for x in range(4):
            for z in range(4):
                for core in range(2):
                    pairs.append((place(*source(y, x, z, core)), place(y, x, z, core)))
    return lax.ppermute(a, ALL, pairs)


def near(a, k):
    return pull(a, lambda y, x, z, c: (y, x + k * c, z + k * (1 - c), c))


def far(a, k):
    return pull(a, lambda y, x, z, c: (y, x + k * (1 - c), z + k * c, c))


def from_y(a, k):
    return pull(a, lambda y, x, z, c: (y + k, x, z, c))


def other_core(a):
    return pull(a, lambda y, x, z, c: (y, x, z, 1 - c))


def outer(left, right):
    return lax.dot_general(left, right, (((1,), (1,)), ((), ())), preferred_element_type=F32)


def inner(left, right):
    return lax.dot_general(left, right, (((0,), (0,)), ((), ())), preferred_element_type=F32)


def dot(left, right):
    return jnp.dot(left, right, preferred_element_type=F32)


def cat(*parts, axis=0):
    return jnp.concatenate(parts, axis=axis)


def together(*arrays):
    return lax.optimization_barrier(arrays)


def blocks_of(parts):
    n = parts[0].shape[0] // 96
    return lambda k: cat(*[p.reshape(n, 4, 24, -1)[:, k] for p in parts], axis=2).reshape(n * 24, 2688)


def first_step(block):
    across = block(2).astype(BF)
    half = (across.shape[0] // 2 + 7) // 8 * 8
    return from_y(across[:half], -1), from_y(across[half:], 1)


def second_step(block, via_up, via_down):
    half = via_up.shape[0]
    up, down = block(1), block(3)
    up = cat((up[:half] + via_up.astype(F32)).astype(BF), up[half:].astype(BF))
    down = cat(down[:half].astype(BF), (down[half:] + via_down.astype(F32)).astype(BF))
    return up, down


def last_step(block, up, down):
    return block(0) + from_y(up, -1).astype(F32) + from_y(down, 1).astype(F32)


def by_row(*blocks):
    rows, width = blocks[0].shape
    return cat(*[b.reshape(rows // 24, 1, 24, width) for b in blocks], axis=1).reshape(rows * 4, width)


def pointwise(total):
    gate, up, hidden_grad = total[:, :896], total[:, 896:1792], total[:, 1792:]
    sigma = jax.nn.sigmoid(gate)
    active = gate * sigma
    hidden = (active * up).astype(BF)
    gate_delta = (hidden_grad * up * sigma * (1.0 + gate * (1.0 - sigma))).astype(BF)
    up_delta = (hidden_grad * active).astype(BF)
    return cat(hidden, gate_delta, up_delta, axis=1)


def spread(a):
    return from_y(a, -1), from_y(a, 1)


def spread_across(before, after):
    half = before.shape[0] // 2
    return cat(from_y(before[:half], -1), from_y(after[half:], 1))


def weight_grads_kernel(tok_ref, delta_ref, gate_ref, up_ref):
    both = inner(tok_ref[...], delta_ref[...])
    half = gate_ref.shape[1]
    gate_ref[...] = both[:, :half].astype(BF)
    up_ref[...] = both[:, half:].astype(BF)


def weight_grads(tok, delta):
    (rows, width), both = tok.shape, delta.shape[1]
    tile = min(width, 512)
    out = jax.ShapeDtypeStruct((width, both // 2), BF)
    return pl.pallas_call(
        weight_grads_kernel,
        grid=(width // tile,),
        in_specs=[pl.BlockSpec((rows, tile), lambda i: (0, i)), pl.BlockSpec((rows, both), lambda i: (0, 0))],
        out_specs=[pl.BlockSpec((tile, both // 2), lambda i: (i, 0))] * 2,
        out_shape=[out, out],
        cost_estimate=pl.CostEstimate(flops=2 * rows * width * both, bytes_accessed=4 * width * both, transcendentals=0),
        compiler_params=pltpu.CompilerParams(vmem_limit_bytes=24 * 2**20),
    )(tok, delta)


def body(tokens, cotangent, gate_weight, up_weight, down_weight):
    y = lax.axis_index("depth")
    width = tokens.shape[1]

    def products(tok, cot):
        return [dot(tok, weights), outer(cot, down_weight)]

    tc = cat(tokens, cotangent)
    weights = cat(gate_weight, up_weight, axis=1)
    near_2, near_1, near_3, weights = together(near(tc, 2), near(tc, 1), near(tc, 3), weights)
    first = jnp.zeros((2, 4, 24, width), BF)
    for k, b in ((2, near_2), (1, near_1), (3, near_3), (0, tc)):
        first = lax.dynamic_update_slice_in_dim(first, b.reshape(2, 1, 24, width), lax.rem(k - y + 4, 4), 1)
    q0 = first.reshape(2, 96, width)
    o0 = other_core(q0)
    q2, q1, q3 = far(q0, 2), far(q0, 1), far(q0, 3)
    tok_0, cot_0 = cat(q0[0], o0[0]), cat(q0[1], o0[1])
    block_0 = blocks_of(products(tok_0, cot_0))
    up_0, down_0 = second_step(block_0, *first_step(block_0))
    q2, q1, q3, up_0, down_0 = together(q2, q1, q3, up_0, down_0)

    tok_a, cot_a = [cat(*[q[n] for q in (q1, q3, q2)]) for n in range(2)]
    tok_b, cot_b = together(other_core(tok_a), other_core(cot_a))
    *part_a, up_0, down_0 = together(*products(tok_a, cot_a), from_y(up_0, -1), from_y(down_0, 1))
    block_a = blocks_of(part_a)
    via_a = first_step(block_a)
    part_b = products(tok_b, cot_b)
    block_b = blocks_of(part_b)
    via_b = first_step(block_b)
    *part_b, via_up, via_down = together(*part_b, *via_a)
    total_0 = block_0(0) + up_0.astype(F32) + down_0.astype(F32)
    up_a, down_a = second_step(block_a, via_up, via_down)
    up_b, down_b = second_step(block_b, *via_b)
    result_0 = pointwise(total_0)
    own = cat(result_0[:24], pointwise(last_step(block_a, up_a, down_a)))
    other = cat(result_0[24:], pointwise(last_step(blocks_of(part_b), up_b, down_b)))

    delta, hidden = cat(own[:, 896:], other[:, 896:]), cat(own[:, :896], other[:, :896])
    before_d, after_d = spread(delta)
    before_d, after_d, hidden = together(before_d, after_d, hidden)
    across_d = spread_across(before_d, after_d)
    delta = by_row(delta, after_d, across_d, before_d)
    before_h, after_h = spread(hidden)
    delta_own, before_h, after_h = together(delta[:384], before_h, after_h)
    hidden = by_row(hidden, after_h, spread_across(before_h, after_h), before_h)

    part_other = other_core(outer(delta[384:], weights).astype(BF))
    part_own, part_other = together(outer(delta_own, weights), part_other)
    part = part_own + part_other.astype(F32)
    part_bf, delta = together(part.astype(BF), delta)
    tok, cot = cat(tok_0[:96], tok_a, tok_0[96:], tok_b), cat(cot_0[:96], cot_a, cot_0[96:], cot_b)
    gate_grad, up_grad = weight_grads(tok, delta)
    gate_grad, up_grad, *parts = together(
        gate_grad, up_grad, *[far(part_bf[96 * n : 96 * n + 96], -k) for n, k in ((3, 2), (1, 1), (2, 3))]
    )
    total = part[:96] + sum(p.astype(F32) for p in parts)
    total, hidden = together(total, hidden)
    down_grad = inner(hidden, cot).astype(BF)

    def block(k):
        return lax.dynamic_slice_in_dim(total, lax.rem(k - y + 4, 4) * 24, 24, 0)

    tokens_grad = block(0) + sum(near(block(k), -k) for k in (2, 1, 3))
    return tokens_grad.astype(BF), gate_grad, up_grad, down_grad


def solution(mesh):
    act, weight, turned = P(("row", "col"), "depth"), P("depth", ("row", "col")), P(("row", "col"), "depth")
    return jax.shard_map(
        body, mesh=mesh, in_specs=(act, act, weight, weight, turned), out_specs=(act, weight, weight, turned), check_vma=False
    )
```

```python
import jax
import jax.numpy as jnp
from jax import lax
from jax.experimental import pallas as pl
from jax.experimental.pallas import tpu as pltpu
from jax.sharding import PartitionSpec as P

ALL = ("depth", "row", "col")
BF = jnp.bfloat16
F32 = jnp.float32


def place(y, x, z, core):
    x, y, z = x % 4, y % 4, z % 4
    return (y * 8 + (x % 2) * 4 + z) * 4 + (x // 2) * 2 + core


def pull(a, source):
    pairs = []
    for y in range(4):
        for x in range(4):
            for z in range(4):
                for core in range(2):
                    pairs.append((place(*source(y, x, z, core)), place(y, x, z, core)))
    return lax.ppermute(a, ALL, pairs)


def near(a, k):
    return pull(a, lambda y, x, z, c: (y, x + k * c, z + k * (1 - c), c))


def far(a, k):
    return pull(a, lambda y, x, z, c: (y, x + k * (1 - c), z + k * c, c))


def from_y(a, k):
    return pull(a, lambda y, x, z, c: (y + k, x, z, c))


def other_core(a):
    return pull(a, lambda y, x, z, c: (y, x, z, 1 - c))


def outer(left, right):
    return lax.dot_general(left, right, (((1,), (1,)), ((), ())), preferred_element_type=F32)


def inner(left, right):
    return lax.dot_general(left, right, (((0,), (0,)), ((), ())), preferred_element_type=F32)


def dot(left, right):
    return jnp.dot(left, right, preferred_element_type=F32)


def cat(*parts, axis=0):
    return jnp.concatenate(parts, axis=axis)


def together(*arrays):
    return lax.optimization_barrier(arrays)


def blocks_of(parts):
    n = parts[0].shape[0] // 96
    return lambda k: cat(*[p.reshape(n, 4, 24, -1)[:, k] for p in parts], axis=2).reshape(n * 24, 2688)


def first_step(block):
    across = block(2).astype(BF)
    half = (across.shape[0] // 2 + 7) // 8 * 8
    return from_y(across[:half], -1), from_y(across[half:], 1)


def second_step(block, via_up, via_down):
    half = via_up.shape[0]
    up, down = block(1), block(3)
    up = cat((up[:half] + via_up.astype(F32)).astype(BF), up[half:].astype(BF))
    down = cat(down[:half].astype(BF), (down[half:] + via_down.astype(F32)).astype(BF))
    return up, down


def last_step(block, up, down):
    return block(0) + from_y(up, -1).astype(F32) + from_y(down, 1).astype(F32)


def by_row(*blocks):
    rows, width = blocks[0].shape
    return cat(*[b.reshape(rows // 24, 1, 24, width) for b in blocks], axis=1).reshape(rows * 4, width)


def pointwise(total):
    gate, up, hidden_grad = total[:, :896], total[:, 896:1792], total[:, 1792:]
    sigma = jax.nn.sigmoid(gate)
    active = gate * sigma
    hidden = (active * up).astype(BF)
    gate_delta = (hidden_grad * up * sigma * (1.0 + gate * (1.0 - sigma))).astype(BF)
    up_delta = (hidden_grad * active).astype(BF)
    return cat(hidden, gate_delta, up_delta, axis=1)


def spread(a):
    return from_y(a, -1), from_y(a, 1)


def spread_across(before, after):
    half = before.shape[0] // 2
    return cat(from_y(before[:half], -1), from_y(after[half:], 1))


def weight_grads_kernel(tok_ref, delta_ref, gate_ref, up_ref):
    both = inner(tok_ref[...], delta_ref[...])
    half = gate_ref.shape[1]
    gate_ref[...] = both[:, :half].astype(BF)
    up_ref[...] = both[:, half:].astype(BF)


def weight_grads(tok, delta):
    (rows, width), both = tok.shape, delta.shape[1]
    tile = min(width, 512)
    out = jax.ShapeDtypeStruct((width, both // 2), BF)
    return pl.pallas_call(
        weight_grads_kernel,
        grid=(width // tile,),
        in_specs=[pl.BlockSpec((rows, tile), lambda i: (0, i)), pl.BlockSpec((rows, both), lambda i: (0, 0))],
        out_specs=[pl.BlockSpec((tile, both // 2), lambda i: (i, 0))] * 2,
        out_shape=[out, out],
        cost_estimate=pl.CostEstimate(flops=2 * rows * width * both, bytes_accessed=4 * width * both, transcendentals=0),
        compiler_params=pltpu.CompilerParams(vmem_limit_bytes=24 * 2**20),
    )(tok, delta)


def body(tokens, cotangent, gate_weight, up_weight, down_weight):
    y = lax.axis_index("depth")
    width = tokens.shape[1]

    def products(tok, cot):
        return [dot(tok, weights), outer(cot, down_weight)]

    low = jnp.array(-jnp.inf, BF)
    rows = tokens.shape[0]
    tc = jnp.maximum(
        lax.pad(tokens, low, ((0, rows, 0), (0, 0, 0))), lax.pad(cotangent, low, ((rows, 0, 0), (0, 0, 0)))
    )
    weights = cat(gate_weight, up_weight, axis=1)
    near_2, near_1, near_3, weights = together(near(tc, 2), near(tc, 1), near(tc, 3), weights)
    chips = [b.reshape(2, 24, width) for b in (tc, near_1, near_2, near_3)]
    first = jnp.stack([lax.select_n(y, *[chips[(n + k) % 4] for k in range(4)]) for n in range(4)], axis=1)
    q0 = first.reshape(2, 96, width)
    o0 = other_core(q0)
    q2, q1, q3 = far(q0, 2), far(q0, 1), far(q0, 3)
    tok_0, cot_0 = cat(q0[0], o0[0]), cat(q0[1], o0[1])
    block_0 = blocks_of(products(tok_0, cot_0))
    up_0, down_0 = second_step(block_0, *first_step(block_0))
    q2, q1, q3, up_0, down_0 = together(q2, q1, q3, up_0, down_0)

    tok_a, cot_a = [cat(*[q[n] for q in (q1, q3, q2)]) for n in range(2)]
    tok_b, cot_b = together(other_core(tok_a), other_core(cot_a))
    *part_a, up_0, down_0 = together(*products(tok_a, cot_a), from_y(up_0, -1), from_y(down_0, 1))
    block_a = blocks_of(part_a)
    via_a = first_step(block_a)
    part_b = products(tok_b, cot_b)
    block_b = blocks_of(part_b)
    via_b = first_step(block_b)
    *part_b, via_up, via_down = together(*part_b, *via_a)
    total_0 = block_0(0) + up_0.astype(F32) + down_0.astype(F32)
    up_a, down_a = second_step(block_a, via_up, via_down)
    up_b, down_b = second_step(block_b, *via_b)
    result_0 = pointwise(total_0)
    own = cat(result_0[:24], pointwise(last_step(block_a, up_a, down_a)))
    other = cat(result_0[24:], pointwise(last_step(blocks_of(part_b), up_b, down_b)))

    delta, hidden = cat(own[:, 896:], other[:, 896:]), cat(own[:, :896], other[:, :896])
    before_d, after_d = spread(delta)
    before_d, after_d, hidden = together(before_d, after_d, hidden)
    across_d = spread_across(before_d, after_d)
    delta = by_row(delta, after_d, across_d, before_d)
    before_h, after_h = spread(hidden)
    delta_own, before_h, after_h = together(delta[:384], before_h, after_h)
    hidden = by_row(hidden, after_h, spread_across(before_h, after_h), before_h)

    part_other = other_core(outer(delta[384:], weights).astype(BF))
    part_own, part_other = together(outer(delta_own, weights), part_other)
    part = part_own + part_other.astype(F32)
    part_bf, delta = together(part.astype(BF), delta)
    tok, cot = cat(tok_0[:96], tok_a, tok_0[96:], tok_b), cat(cot_0[:96], cot_a, cot_0[96:], cot_b)
    gate_grad, up_grad = weight_grads(tok, delta)
    gate_grad, up_grad, *parts = together(
        gate_grad, up_grad, *[far(part_bf[96 * n : 96 * n + 96], -k) for n, k in ((3, 2), (1, 1), (2, 3))]
    )
    total = part[:96] + sum(p.astype(F32) for p in parts)
    total, hidden = together(total, hidden)
    down_grad = inner(hidden, cot).astype(BF)

    def block(k):
        return lax.dynamic_slice_in_dim(total, lax.rem(k - y + 4, 4) * 24, 24, 0)

    tokens_grad = block(0) + sum(near(block(k), -k) for k in (2, 1, 3))
    return tokens_grad.astype(BF), gate_grad, up_grad, down_grad


def solution(mesh):
    act, weight, turned = P(("row", "col"), "depth"), P("depth", ("row", "col")), P(("row", "col"), "depth")
    return jax.shard_map(
        body, mesh=mesh, in_specs=(act, act, weight, weight, turned), out_specs=(act, weight, weight, turned), check_vma=False
    )
```
